32 devices in a mesh: groups: 2 (over x), aux: 16 (over z, y, core).
Axes of the slice: x: 2, y: 2, z: 4, core: 2. Of those that a mesh axis runs over, the one named last changes fastest.
Arguments:
- coefficients: float32 [32, 256, 4096], P(('groups', 'aux')), parts along dimension 0, may hold values from -0.5 to 0.5
- screening: int32 [2, 32, 256], P(None, ('groups', 'aux')), parts along dimension 1, may hold values from 0 to 127, as said below
- kept_count: int32 [32], P(('groups', 'aux')), parts along dimension 0, may hold values from 1 to 256, 2048 in all
- occupied: float32 [16384, 125], P(('groups', 'aux')), parts along dimension 0, may hold values from -0.5 to 0.5
- owner_order: int32 [256], P('groups'), parts along dimension 0, may hold values from 0 to 127, each once
Outputs:
- k_panel: float32 [256, 64, 1024], P(('groups', 'aux')), parts along dimension 0
The draws below stay inside these ranges and needn't reach their ends.
There are 2 independent parts, one for each index of `groups`. The reference program is written for one: setup_inputs(seed, part) draws one part's arguments, and reference() takes and returns one part's arrays. A program takes and returns all parts, laid end to end along the dimension named above; each array names one. Nothing has to cross between parts.
Inputs may be any that keep to these rules, and one draw needn't show every extreme that they name: Block indices of the screening list; the pairs of one auxiliary function are distinct. `kept_count`: the live slots of one part's 16 functions sum to 2048.
All inputs are finite; a program needn't handle non-finite values. No bound on the sum of `kept_count` on one device may be relied on, other than what follows from the above.
Results may differ from the reference program's by a relative error of at most 0.0003.
Values sent between devices are 32-bit elements; how exact they have to be, the bound alone decides.
A program may use at most 128 MiB of HBM per device.

```python
import math
import jax
import jax.numpy as jnp
import numpy as np
from jax import lax

BLK = 64
NBLK = 128
NOCC = 125
KEPT = 256
NBF = 8192
PANEL = 1024
AUX = 16


def draw_screening(key, part):
    key = jax.random.fold_in(key, 11)
    keys = jax.random.split(key, AUX)

    def one_function(single_key):
        return jax.random.permutation(single_key, NBLK * NBLK)[:KEPT]
    picked = jax.vmap(one_function)(keys).astype(jnp.int32)
    return jnp.stack([picked // NBLK, picked % NBLK]).astype(jnp.int32)


def levels(rng, dims, cuts, least, high):
    def one(position, parts):
        steps = jax.random.uniform(jax.random.fold_in(jax.random.fold_in(rng, 6), position), (parts,), jnp.float32, least / len(cuts), high / len(cuts))
        return jnp.repeat(jnp.exp(steps), dims[position] // parts).reshape((-1,) + (1,) * (len(dims) - position - 1))

    factor_of = one(*cuts[0])
    for cut in cuts[1:]:
        factor_of = factor_of * one(*cut)
    return factor_of


def split_up(count, total, bound, lean):
    portions = [(1 << 20) // math.isqrt(grade ** lean) + 1 for grade in range(2, count + 1)]
    surplus, holding = total - bound - (count - 1), [1] * (count - 1)
    while surplus > 0:
        movable = [i for i in range(count - 1) if holding[i] < bound]
        pool, left = sum([portions[i] for i in movable]), surplus
        for i in movable:
            more = min(bound - holding[i], max(1, left * portions[i] // pool), surplus)
            holding[i] = holding[i] + more
            surplus = surplus - more
    return np.array([bound] + holding)


def uneven_parts(rng, count, total, bound, lean):
    if count == 2:
        one = jax.random.randint(rng, (), max(1, total - bound), min(bound, total - 1) + 1)
        return jnp.stack([one, total - one])
    sizes = jnp.asarray(split_up(count, total, bound, lean), jnp.int32)
    pairs = (count - 1) // 2
    giver, receiver = sizes[1:1 + 2 * pairs:2], sizes[2:2 + 2 * pairs:2]
    slack = jnp.minimum(giver - 1, bound - receiver)
    moved = jax.random.randint(jax.random.fold_in(rng, 1), (pairs,), 0, 1 << 20) % (slack + 1)
    sizes = sizes.at[1:1 + 2 * pairs:2].set(giver - moved).at[2:2 + 2 * pairs:2].set(receiver + moved)
    return sizes[jax.random.permutation(jax.random.fold_in(rng, 2), count)]


def centred(stream_key, dims, spread, most, cuts=(), kind=jnp.bfloat16):
    values = jax.random.normal(stream_key, dims, jnp.float32) * spread
    if len(cuts) > 0:
        values = levels(stream_key, dims, cuts, -0.22, 0.18) * values
    return jnp.clip(values, min=-most, max=most).astype(kind)


def setup_inputs(seed: int = 0, part: int = 0) -> dict:
    streams_of = jax.random.split(jax.random.key(seed), 6)
    part_splits = jax.random.split(jax.random.fold_in(streams_of[5], part), 6)
    coefficients = centred(part_splits[0], (AUX, KEPT, BLK * BLK), (KEPT * BLK // NBLK) ** -0.5, 0.5, ((0, 16),), jnp.float32)
    screening = draw_screening(jax.random.fold_in(jax.random.fold_in(streams_of[5], part), 71), part)
    kept_count = uneven_parts(part_splits[2], AUX, AUX * KEPT // 2, KEPT, 2).astype(jnp.int32)
    occupied = centred(part_splits[3], (NBF, NOCC), NOCC ** -0.5, 0.5, ((0, 16),), jnp.float32)
    owner_order = jax.random.permutation(part_splits[4], NBLK).astype(jnp.int32)
    return {"coefficients": coefficients, "screening": screening, "kept_count": kept_count, "occupied": occupied, "owner_order": owner_order}


HIGHEST = lax.Precision.HIGHEST


def reference(coefficients, screening, kept_count, occupied, owner_order):
    blocks = occupied.reshape(NBLK, BLK, NOCC)
    slot_index = jnp.arange(KEPT, dtype=jnp.int32)

    def one_function(running, inputs):
        flat_tiles, row_blocks, col_blocks, live_count = inputs
        tile_values = flat_tiles.reshape(KEPT, BLK, BLK)
        live_mask = (slot_index < live_count).astype(jnp.float32)
        products = jnp.einsum("tmn,tni->tmi", tile_values, blocks[col_blocks], precision=HIGHEST)
        products = products * live_mask[:, None, None]
        half_done = jax.ops.segment_sum(products, row_blocks, num_segments=NBLK).reshape(NBLK * BLK, NOCC)
        panel_half = half_done[:PANEL]
        return running + jnp.einsum("ri,li->rl", half_done, panel_half, precision=HIGHEST), None

    running = jnp.zeros((NBLK * BLK, PANEL), jnp.float32)
    exchange_full, _ = lax.scan(one_function, running, (coefficients, screening[0], screening[1], kept_count))
    return exchange_full.reshape(NBLK, BLK, PANEL)[owner_order]
```

```python
import functools

import jax
import jax.numpy as jnp
from jax import lax
from jax.experimental import pallas as pl
from jax.experimental.pallas import tpu as pltpu
from jax.sharding import PartitionSpec as P

BLK = 64
PBLK = 16
LANES = 128
GROUP = 8
TILE = 256
VMEM_BYTES = 56 * 2**20
MESH_ID = pl.DeviceIdType.MESH


def halves(x):
    high = x.astype(jnp.bfloat16)
    low = (x - high.astype(jnp.float32)).astype(jnp.bfloat16)
    return high, low


def half_kernel(block_count, occ, kept_ref, rows_ref, cols_ref, place_ref, tiles_ref, orbitals_ref, half_ref, panel_ref, weights):
    @pl.loop(0, block_count)
    def _(b):
        high, low = halves(orbitals_ref[b])
        pad = jnp.zeros((BLK, LANES - occ), jnp.bfloat16)
        high = jnp.concatenate([high, pad], axis=1)
        low = jnp.concatenate([low, pad], axis=1)
        weights[b] = jnp.concatenate([high, high, low, low], axis=0)
        half_ref[b] = jnp.zeros((BLK, LANES), jnp.float32)

    half_ref[block_count] = jnp.zeros((BLK, LANES), jnp.float32)
    live = kept_ref[0]

    @pl.loop(0, (live + GROUP - 1) // GROUP)
    def _(g):
        products = []
        for u in range(GROUP):
            t = g * GROUP + u
            tile = tiles_ref[t]
            lhs = jnp.concatenate([tile, tile], axis=1)
            products.append(jnp.dot(lhs, weights[cols_ref[t]], preferred_element_type=jnp.float32))
        for u in range(GROUP):
            t = g * GROUP + u
            place = jnp.where(t < live, place_ref[rows_ref[t]], block_count)
            half_ref[place] += products[u]

    for a in range(PBLK):
        panel_ref[pl.ds(a * BLK, BLK), :] = half_ref[place_ref[a]]


def exchange_kernel(shape, half_ref, panel_ref, out_ref, arrived, panels, lhs, a_send, a_recv, z_send, y_send, c_send, p_recv, local_sem):
    nz, ny, n = shape
    owned = arrived.shape[1]
    me = lax.axis_index("aux")
    z, y, c = me // (2 * ny), (me // 2) % ny, me % 2

    def index(zz, yy, cc):
        return (zz * ny + yy) * 2 + cc

    def partner(i):
        k = lax.rem(i // (2 * ny) + nz // 2, nz)
        return k, lax.rem(i // 2, ny), lax.rem(i, 2)

    def send_to(i):
        k, dy, dc = partner(i)
        return index(lax.rem(z + k, nz), lax.rem(y + dy, ny), lax.rem(c + dc, 2))

    def recv_from(i):
        k, dy, dc = partner(i)
        return index(lax.rem(z - k + nz, nz), lax.rem(y - dy + ny, ny), lax.rem(c - dc + 2, 2))

    barrier = pltpu.get_barrier_semaphore()

    @pl.loop(1, n)
    def _(k):
        pl.semaphore_signal(barrier, inc=1, device_id={"aux": lax.rem(me + k, n)}, device_id_type=MESH_ID)

    pl.semaphore_wait(barrier, n - 1)

    def panel_copy(q, dst, sem, own=False):
        return pltpu.make_async_remote_copy(
            src_ref=panel_ref if own else panels.at[q],
            dst_ref=panels.at[q],
            send_sem=sem,
            recv_sem=p_recv.at[q],
            device_id={"aux": dst},
            device_id_type=MESH_ID,
        )

    def row_copy(dst, slot):
        return pltpu.make_async_remote_copy(
            src_ref=half_ref.at[pl.ds(dst * owned, owned)],
            dst_ref=arrived.at[slot],
            send_sem=a_send.at[dst],
            recv_sem=a_recv.at[slot],
            device_id={"aux": dst},
            device_id_type=MESH_ID,
        )

    def wait_panel(q):
        panel_copy(q, me, c_send.at[q]).wait_recv()

    up, down = index(z + 1, y, c), index(z - 1, y, c)
    other_y, other_c = index(z, ny - 1 - y, c), index(z, y, 1 - c)

    def spread(q, own=False):
        if ny > 1:
            panel_copy(q, other_y, y_send.at[q], own).start()
        panel_copy(q, other_c, c_send.at[q], own).start()

    @pl.when(z < nz - 1)
    def _():
        panel_copy(me, up, z_send.at[0, me], True).start()

    @pl.when(z > 0)
    def _():
        panel_copy(me, down, z_send.at[1, me], True).start()

    spread(me, True)
    own_panel = pltpu.make_async_copy(panel_ref, panels.at[me], local_sem.at[0])
    own_rows = pltpu.make_async_copy(half_ref.at[pl.ds(me * owned, owned)], arrived.at[me], local_sem.at[1])
    own_panel.start()
    own_rows.start()

    @pl.loop(0, n)
    def _(i):
        dst = send_to(i)

        @pl.when(dst != me)
        def _():
            row_copy(dst, me).start()

    def from_y(zz):
        if ny > 1:
            q = index(zz, ny - 1 - y, c)
            wait_panel(q)
            panel_copy(q, other_c, c_send.at[q]).start()

    from_y(z)

    @pl.loop(1, nz)
    def _(d):
        @pl.when(z - d >= 0)
        def _():
            q = index(z - d, y, c)
            wait_panel(q)

            @pl.when(z < nz - 1)
            def _():
                panel_copy(q, up, z_send.at[0, q]).start()

            spread(q)

        @pl.when(z + d < nz)
        def _():
            q = index(z + d, y, c)
            wait_panel(q)

            @pl.when(z > 0)
            def _():
                panel_copy(q, down, z_send.at[1, q]).start()

            spread(q)

        @pl.when(z - d >= 0)
        def _():
            from_y(z - d)

        @pl.when(z + d < nz)
        def _():
            from_y(z + d)

    @pl.loop(0, nz * ny)
    def _(j):
        wait_panel(2 * j + 1 - c)

    own_panel.wait()
    own_rows.wait()
    out_ref[...] = jnp.zeros_like(out_ref)
    rows = owned * BLK
    width = out_ref.shape[1]

    @pl.loop(0, n)
    def _(i):
        q = recv_from(i)

        @pl.when(q != me)
        def _():
            row_copy(me, q).wait_recv()

        high, low = halves(arrived[q].reshape(rows, LANES))
        lhs[...] = jnp.concatenate([high, high, low], axis=1)

        @pl.loop(0, width // TILE)
        def _(j):
            start = pl.multiple_of(j * TILE, TILE)
            p_high, p_low = halves(panels[q, pl.ds(start, TILE), :])
            rhs = jnp.concatenate([p_high, p_low, p_high], axis=1)
            out_ref[:, pl.ds(start, TILE)] += lax.dot_general(
                lhs[...], rhs, (((1,), (1,)), ((), ())), preferred_element_type=jnp.float32
            )

    @pl.loop(0, n)
    def _(i):
        dst = send_to(i)

        @pl.when(dst != me)
        def _():
            row_copy(dst, me).wait_send()

    @pl.loop(0, nz)
    def _(zz):
        q = index(zz, y, c)

        @pl.when((zz <= z) & (z < nz - 1))
        def _():
            panel_copy(q, up, z_send.at[0, q]).wait_send()

        @pl.when((zz >= z) & (z > 0))
        def _():
            panel_copy(q, down, z_send.at[1, q]).wait_send()

        if ny > 1:
            panel_copy(q, other_y, y_send.at[q]).wait_send()

    @pl.loop(0, nz * ny)
    def _(j):
        q = 2 * j + c
        panel_copy(q, other_c, c_send.at[q]).wait_send()


def shards(coefficients, screening, kept_count, occupied, owner_order):
    slot_count = coefficients.shape[1]
    occ = occupied.shape[1]
    n = lax.axis_size("aux")
    orbitals = lax.all_gather(occupied, "aux", axis=0, tiled=True)
    block_count = orbitals.shape[0] // BLK
    owned = block_count // n
    width = PBLK * BLK
    high, low = halves(coefficients[0].reshape(slot_count, BLK, BLK))
    tiles = jnp.concatenate([high, low], axis=-1)
    place = jnp.zeros((block_count,), jnp.int32).at[owner_order].set(jnp.arange(block_count, dtype=jnp.int32))
    smem = pl.BlockSpec(memory_space=pltpu.SMEM)
    vmem = pl.BlockSpec(memory_space=pltpu.VMEM)
    anyw = pl.BlockSpec(memory_space=pl.ANY)
    half, panel = pl.pallas_call(
        functools.partial(half_kernel, block_count, occ),
        out_shape=(
            jax.ShapeDtypeStruct((block_count + 1, BLK, LANES), jnp.float32),
            jax.ShapeDtypeStruct((width, LANES), jnp.float32),
        ),
        in_specs=[smem] * 4 + [vmem] * 2,
        out_specs=(vmem, vmem),
        scratch_shapes=[pltpu.VMEM((block_count, 4 * BLK, LANES), jnp.bfloat16)],
        compiler_params=pltpu.CompilerParams(vmem_limit_bytes=VMEM_BYTES),
    )(kept_count, screening[0, 0], screening[1, 0], place, tiles, orbitals.reshape(block_count, BLK, occ))

    ny = 2 if n == 16 else 1
    nz = n // (2 * ny)
    dma = pltpu.SemaphoreType.DMA
    rows = owned * BLK
    out = pl.pallas_call(
        functools.partial(exchange_kernel, (nz, ny, n)),
        out_shape=jax.ShapeDtypeStruct((rows, width), jnp.float32),
        in_specs=[anyw, anyw],
        out_specs=vmem,
        scratch_shapes=[
            pltpu.VMEM((n, owned, BLK, LANES), jnp.float32),
            pltpu.VMEM((n, width, LANES), jnp.float32),
            pltpu.VMEM((rows, 3 * LANES), jnp.bfloat16),
            dma((n,)), dma((n,)), dma((2, n)), dma((n,)), dma((n,)), dma((n,)), dma((2,)),
        ],
        compiler_params=pltpu.CompilerParams(collective_id=0, has_side_effects=True, vmem_limit_bytes=VMEM_BYTES),
    )(half, panel)
    return out.reshape(owned, BLK, width)


def solution(mesh):
    return jax.shard_map(
        shards,
        mesh=mesh,
        in_specs=(
            P(("groups", "aux"), None, None),
            P(None, ("groups", "aux"), None),
            P(("groups", "aux")),
            P(("groups", "aux"), None),
            P("groups"),
        ),
        out_specs=P(("groups", "aux"), None, None),
        check_vma=False,
    )
```

```python
import functools

import jax
import jax.numpy as jnp
from jax import lax
from jax.experimental import pallas as pl
from jax.experimental.pallas import tpu as pltpu
from jax.sharding import PartitionSpec as P

BLK = 64
PBLK = 16
LANES = 128
GROUP = 8
TILE = 256
VMEM_BYTES = 56 * 2**20
MESH_ID = pl.DeviceIdType.MESH


def halves(x):
    high = x.astype(jnp.bfloat16)
    low = (x - high.astype(jnp.float32)).astype(jnp.bfloat16)
    return high, low


def half_kernel(block_count, kept_ref, rows_ref, cols_ref, place_ref, tiles_ref, orbitals_ref, half_ref, panel_ref, weights):
    @pl.loop(0, block_count)
    def _(b):
        high, low = halves(orbitals_ref[b])
        weights[b] = jnp.concatenate([high, high, low, low], axis=0)
        half_ref[b] = jnp.zeros((BLK, LANES), jnp.float32)

    half_ref[block_count] = jnp.zeros((BLK, LANES), jnp.float32)
    live = kept_ref[0]

    @pl.loop(0, (live + GROUP - 1) // GROUP)
    def _(g):
        products = []
        for u in range(GROUP):
            t = g * GROUP + u
            tile = tiles_ref[t]
            lhs = jnp.concatenate([tile, tile], axis=1)
            products.append(jnp.dot(lhs, weights[cols_ref[t]], preferred_element_type=jnp.float32))
        for u in range(GROUP):
            t = g * GROUP + u
            place = jnp.where(t < live, place_ref[rows_ref[t]], block_count)
            for parity in range(2):
                part = products[u][parity * (BLK // 2):(parity + 1) * (BLK // 2)]
                half_ref[place, pl.ds(parity, BLK // 2, stride=2), :] += part

    for a in range(PBLK):
        panel_ref[pl.ds(a * BLK, BLK), :] = half_ref[place_ref[a]]


def spread_kernel(shape, coefficients_ref, shard_ref, tiles_ref, gathered, z_send, y_send, c_send, recv, local_sem):
    nz, ny, n = shape
    me = lax.axis_index("aux")
    z, y, c = me // (2 * ny), (me // 2) % ny, me % 2

    def index(zz, yy, cc):
        return (zz * ny + yy) * 2 + cc

    barrier = pltpu.get_barrier_semaphore()

    @pl.loop(1, n)
    def _(k):
        pl.semaphore_signal(barrier, inc=1, device_id={"aux": lax.rem(me + k, n)}, device_id_type=MESH_ID)

    pl.semaphore_wait(barrier, n - 1)

    def copy(q, dst, sem, own=False):
        return pltpu.make_async_remote_copy(
            src_ref=shard_ref if own else gathered.at[q],
            dst_ref=gathered.at[q],
            send_sem=sem,
            recv_sem=recv.at[q],
            device_id={"aux": dst},
            device_id_type=MESH_ID,
        )

    up, down = index(z + 1, y, c), index(z - 1, y, c)
    other_y, other_c = index(z, ny - 1 - y, c), index(z, y, 1 - c)

    def wait(q):
        copy(q, other_c, c_send.at[q]).wait_recv()

    def spread(q, own=False):
        if ny > 1:
            copy(q, other_y, y_send.at[q], own).start()
        copy(q, other_c, c_send.at[q], own).start()

    @pl.when(z < nz - 1)
    def _():
        copy(me, up, z_send.at[0, me], True).start()

    @pl.when(z > 0)
    def _():
        copy(me, down, z_send.at[1, me], True).start()

    spread(me, True)
    own_shard = pltpu.make_async_copy(shard_ref, gathered.at[me], local_sem)
    own_shard.start()

    slots = tiles_ref.shape[0] // nz
    group = min(GROUP, slots)

    def prepare(part):
        @pl.loop(0, slots // group)
        def _(g):
            for u in range(group):
                t = part * slots + g * group + u
                tile = coefficients_ref[t]
                high = tile.astype(jnp.bfloat16).astype(jnp.float32)
                low = tile - high
                first = lax.broadcasted_iota(jnp.int32, tile.shape, 1) < BLK
                even = jnp.where(first, high, pltpu.roll(low, BLK, 1))
                odd = jnp.where(first, pltpu.roll(high, BLK, 1), low)
                tiles_ref[t] = jnp.concatenate([even, odd], axis=0).astype(jnp.bfloat16)

    def from_y(zz):
        if ny > 1:
            q = index(zz, ny - 1 - y, c)
            wait(q)
            copy(q, other_c, c_send.at[q]).start()

    prepare(0)

    @pl.loop(1, nz)
    def _(d):
        @pl.when(z - d >= 0)
        def _():
            q = index(z - d, y, c)
            wait(q)

            @pl.when(z < nz - 1)
            def _():
                copy(q, up, z_send.at[0, q]).start()

            spread(q)

        @pl.when(z + d < nz)
        def _():
            q = index(z + d, y, c)
            wait(q)

            @pl.when(z > 0)
            def _():
                copy(q, down, z_send.at[1, q]).start()

            spread(q)

        prepare(d)

    @pl.loop(0, nz)
    def _(d):
        @pl.when(z - d >= 0)
        def _():
            from_y(z - d)

        @pl.when((z + d < nz) & (d > 0))
        def _():
            from_y(z + d)

    @pl.loop(0, nz * ny)
    def _(j):
        wait(2 * j + 1 - c)

    own_shard.wait()

    @pl.loop(0, nz)
    def _(zz):
        q = index(zz, y, c)

        @pl.when((zz <= z) & (z < nz - 1))
        def _():
            copy(q, up, z_send.at[0, q]).wait_send()

        @pl.when((zz >= z) & (z > 0))
        def _():
            copy(q, down, z_send.at[1, q]).wait_send()

        if ny > 1:
            copy(q, other_y, y_send.at[q]).wait_send()

    @pl.loop(0, nz * ny)
    def _(j):
        q = 2 * j + c
        copy(q, other_c, c_send.at[q]).wait_send()


def exchange_kernel(shape, half_ref, panel_ref, out_ref, arrived, panels, lhs, a_send, a_recv, z_send, y_send, c_send, p_recv, local_sem):
    nz, ny, n = shape
    owned = arrived.shape[1]
    me = lax.axis_index("aux")
    z, y, c = me // (2 * ny), (me // 2) % ny, me % 2

    def index(zz, yy, cc):
        return (zz * ny + yy) * 2 + cc

    def partner(i):
        k = lax.rem(i // (2 * ny) + nz // 2, nz)
        return k, lax.rem(i // 2, ny), lax.rem(i, 2)

    def send_to(i):
        k, dy, dc = partner(i)
        return index(lax.rem(z + k, nz), lax.rem(y + dy, ny), lax.rem(c + dc, 2))

    def recv_from(i):
        k, dy, dc = partner(i)
        return index(lax.rem(z - k + nz, nz), lax.rem(y - dy + ny, ny), lax.rem(c - dc + 2, 2))

    barrier = pltpu.get_barrier_semaphore()

    @pl.loop(1, n)
    def _(k):
        pl.semaphore_signal(barrier, inc=1, device_id={"aux": lax.rem(me + k, n)}, device_id_type=MESH_ID)

    pl.semaphore_wait(barrier, n - 1)

    def panel_copy(q, dst, sem, own=False):
        return pltpu.make_async_remote_copy(
            src_ref=panel_ref if own else panels.at[q],
            dst_ref=panels.at[q],
            send_sem=sem,
            recv_sem=p_recv.at[q],
            device_id={"aux": dst},
            device_id_type=MESH_ID,
        )

    def row_copy(dst, slot):
        return pltpu.make_async_remote_copy(
            src_ref=half_ref.at[pl.ds(dst * owned, owned)],
            dst_ref=arrived.at[slot],
            send_sem=a_send.at[dst],
            recv_sem=a_recv.at[slot],
            device_id={"aux": dst},
            device_id_type=MESH_ID,
        )

    def wait_panel(q):
        panel_copy(q, me, c_send.at[q]).wait_recv()

    up, down = index(z + 1, y, c), index(z - 1, y, c)
    other_y, other_c = index(z, ny - 1 - y, c), index(z, y, 1 - c)

    def spread(q, own=False):
        if ny > 1:
            panel_copy(q, other_y, y_send.at[q], own).start()
        panel_copy(q, other_c, c_send.at[q], own).start()

    @pl.when(z < nz - 1)
    def _():
        panel_copy(me, up, z_send.at[0, me], True).start()

    @pl.when(z > 0)
    def _():
        panel_copy(me, down, z_send.at[1, me], True).start()

    spread(me, True)
    own_panel = pltpu.make_async_copy(panel_ref, panels.at[me], local_sem.at[0])
    own_rows = pltpu.make_async_copy(half_ref.at[pl.ds(me * owned, owned)], arrived.at[me], local_sem.at[1])
    own_panel.start()
    own_rows.start()

    @pl.loop(0, n)
    def _(i):
        dst = send_to(i)

        @pl.when(dst != me)
        def _():
            row_copy(dst, me).start()

    def from_y(zz):
        if ny > 1:
            q = index(zz, ny - 1 - y, c)
            wait_panel(q)
            panel_copy(q, other_c, c_send.at[q]).start()

    from_y(z)

    @pl.loop(1, nz)
    def _(d):
        @pl.when(z - d >= 0)
        def _():
            q = index(z - d, y, c)
            wait_panel(q)

            @pl.when(z < nz - 1)
            def _():
                panel_copy(q, up, z_send.at[0, q]).start()

            spread(q)

        @pl.when(z + d < nz)
        def _():
            q = index(z + d, y, c)
            wait_panel(q)

            @pl.when(z > 0)
            def _():
                panel_copy(q, down, z_send.at[1, q]).start()

            spread(q)

        @pl.when(z - d >= 0)
        def _():
            from_y(z - d)

        @pl.when(z + d < nz)
        def _():
            from_y(z + d)

    @pl.loop(0, nz * ny)
    def _(j):
        wait_panel(2 * j + 1 - c)

    own_panel.wait()
    own_rows.wait()
    out_ref[...] = jnp.zeros_like(out_ref)
    rows = owned * BLK
    width = out_ref.shape[1]

    @pl.loop(0, n)
    def _(i):
        q = recv_from(i)

        @pl.when(q != me)
        def _():
            row_copy(me, q).wait_recv()

        high, low = halves(arrived[q].reshape(rows, LANES))
        lhs[...] = jnp.concatenate([high, high, low], axis=1)

        @pl.loop(0, width // TILE)
        def _(j):
            start = pl.multiple_of(j * TILE, TILE)
            p_high, p_low = halves(panels[q, pl.ds(start, TILE), :])
            rhs = jnp.concatenate([p_high, p_low, p_high], axis=1)
            out_ref[:, pl.ds(start, TILE)] += lax.dot_general(
                lhs[...], rhs, (((1,), (1,)), ((), ())), preferred_element_type=jnp.float32
            )

    @pl.loop(0, n)
    def _(i):
        dst = send_to(i)

        @pl.when(dst != me)
        def _():
            row_copy(dst, me).wait_send()

    @pl.loop(0, nz)
    def _(zz):
        q = index(zz, y, c)

        @pl.when((zz <= z) & (z < nz - 1))
        def _():
            panel_copy(q, up, z_send.at[0, q]).wait_send()

        @pl.when((zz >= z) & (z > 0))
        def _():
            panel_copy(q, down, z_send.at[1, q]).wait_send()

        if ny > 1:
            panel_copy(q, other_y, y_send.at[q]).wait_send()

    @pl.loop(0, nz * ny)
    def _(j):
        q = 2 * j + c
        panel_copy(q, other_c, c_send.at[q]).wait_send()


def shards(coefficients, screening, kept_count, occupied, owner_order):
    slot_count = coefficients.shape[1]
    occ = occupied.shape[1]
    n = lax.axis_size("aux")
    shard_rows = occupied.shape[0]
    block_count = shard_rows * n // BLK
    owned = block_count // n
    width = PBLK * BLK
    ny = 2 if n == 16 else 1
    nz = n // (2 * ny)
    dma = pltpu.SemaphoreType.DMA
    place = jnp.zeros((block_count,), jnp.int32).at[owner_order].set(jnp.arange(block_count, dtype=jnp.int32))
    smem = pl.BlockSpec(memory_space=pltpu.SMEM)
    vmem = pl.BlockSpec(memory_space=pltpu.VMEM)
    anyw = pl.BlockSpec(memory_space=pl.ANY)
    flat = BLK * BLK // LANES
    tiles, orbitals = pl.pallas_call(
        functools.partial(spread_kernel, (nz, ny, n)),
        out_shape=(
            jax.ShapeDtypeStruct((slot_count, BLK, LANES), jnp.bfloat16),
            jax.ShapeDtypeStruct((n, shard_rows, LANES), jnp.float32),
        ),
        in_specs=[vmem, anyw],
        out_specs=(vmem, anyw),
        scratch_shapes=[dma((2, n)), dma((n,)), dma((n,)), dma((n,)), dma],
        compiler_params=pltpu.CompilerParams(collective_id=1, has_side_effects=True, vmem_limit_bytes=VMEM_BYTES),
    )(coefficients[0].reshape(slot_count, flat, LANES), jnp.pad(occupied, ((0, 0), (0, LANES - occ))))
    half, panel = pl.pallas_call(
        functools.partial(half_kernel, block_count),
        out_shape=(
            jax.ShapeDtypeStruct((block_count + 1, BLK, LANES), jnp.float32),
            jax.ShapeDtypeStruct((width, LANES), jnp.float32),
        ),
        in_specs=[smem] * 4 + [vmem] * 2,
        out_specs=(vmem, vmem),
        scratch_shapes=[pltpu.VMEM((block_count, 4 * BLK, LANES), jnp.bfloat16)],
        compiler_params=pltpu.CompilerParams(vmem_limit_bytes=VMEM_BYTES),
    )(kept_count, screening[0, 0], screening[1, 0], place, tiles, orbitals.reshape(block_count, BLK, LANES))

    rows = owned * BLK
    out = pl.pallas_call(
        functools.partial(exchange_kernel, (nz, ny, n)),
        out_shape=jax.ShapeDtypeStruct((rows, width), jnp.float32),
        in_specs=[anyw, anyw],
        out_specs=vmem,
        scratch_shapes=[
            pltpu.VMEM((n, owned, BLK, LANES), jnp.float32),
            pltpu.VMEM((n, width, LANES), jnp.float32),
            pltpu.VMEM((rows, 3 * LANES), jnp.bfloat16),
            dma((n,)), dma((n,)), dma((2, n)), dma((n,)), dma((n,)), dma((n,)), dma((2,)),
        ],
        compiler_params=pltpu.CompilerParams(collective_id=0, has_side_effects=True, vmem_limit_bytes=VMEM_BYTES),
    )(half, panel)
    return out.reshape(owned, BLK, width)


def solution(mesh):
    return jax.shard_map(
        shards,
        mesh=mesh,
        in_specs=(
            P(("groups", "aux"), None, None),
            P(None, ("groups", "aux"), None),
            P(("groups", "aux")),
            P(("groups", "aux"), None),
            P("groups"),
        ),
        out_specs=P(("groups", "aux"), None, None),
        check_vma=False,
    )
```

```python
import functools

import jax
import jax.numpy as jnp
from jax import lax
from jax.experimental import pallas as pl
from jax.experimental.pallas import tpu as pltpu
from jax.sharding import PartitionSpec as P

BLK = 64
PBLK = 16
LANES = 128
GROUP = 8
TILE = 256
VMEM_BYTES = 56 * 2**20
MESH_ID = pl.DeviceIdType.MESH


def halves(x):
    high = x.astype(jnp.bfloat16)
    low = (x - high.astype(jnp.float32)).astype(jnp.bfloat16)
    return high, low


def half_kernel(block_count, kept_ref, rows_ref, cols_ref, place_ref, tiles_ref, orbitals_ref, half_ref, panel_ref, weights):
    @pl.loop(0, block_count)
    def _(b):
        high, low = halves(orbitals_ref[b])
        weights[b] = jnp.concatenate([high, high, low, low], axis=0)
        half_ref[b] = jnp.zeros((BLK, LANES), jnp.float32)

    half_ref[block_count] = jnp.zeros((BLK, LANES), jnp.float32)
    live = kept_ref[0]

    @pl.loop(0, (live + GROUP - 1) // GROUP)
    def _(g):
        products = []
        for u in range(GROUP):
            t = g * GROUP + u
            tile = tiles_ref[t]
            lhs = jnp.concatenate([tile, tile], axis=1)
            products.append(jnp.dot(lhs, weights[cols_ref[t]], preferred_element_type=jnp.float32))
        for u in range(GROUP):
            t = g * GROUP + u
            place = jnp.where(t < live, place_ref[rows_ref[t]], block_count)
            for parity in range(2):
                part = products[u][parity * (BLK // 2):(parity + 1) * (BLK // 2)]
                half_ref[place, pl.ds(parity, BLK // 2, stride=2), :] += part

    for a in range(0, PBLK, 2):
        pair = jnp.concatenate([half_ref[place_ref[a]], half_ref[place_ref[a + 1]]], axis=0)
        panel_ref[:, pl.ds(a * BLK, 2 * BLK)] = pair.T


def spread_kernel(shape, coefficients_ref, shard_ref, tiles_ref, gathered, z_send, y_send, c_send, recv, local_sem):
    nz, ny, n = shape
    me = lax.axis_index("aux")
    z, y, c = me // (2 * ny), (me // 2) % ny, me % 2

    def index(zz, yy, cc):
        return (zz * ny + yy) * 2 + cc

    barrier = pltpu.get_barrier_semaphore()

    @pl.loop(1, n)
    def _(k):
        pl.semaphore_signal(barrier, inc=1, device_id={"aux": lax.rem(me + k, n)}, device_id_type=MESH_ID)

    pl.semaphore_wait(barrier, n - 1)

    def copy(q, dst, sem, own=False):
        return pltpu.make_async_remote_copy(
            src_ref=shard_ref if own else gathered.at[q],
            dst_ref=gathered.at[q],
            send_sem=sem,
            recv_sem=recv.at[q],
            device_id={"aux": dst},
            device_id_type=MESH_ID,
        )

    up, down = index(z + 1, y, c), index(z - 1, y, c)
    other_y, other_c = index(z, ny - 1 - y, c), index(z, y, 1 - c)

    def wait(q):
        copy(q, other_c, c_send.at[q]).wait_recv()

    def spread(q, own=False):
        if ny > 1:
            copy(q, other_y, y_send.at[q], own).start()
        copy(q, other_c, c_send.at[q], own).start()

    @pl.when(z < nz - 1)
    def _():
        copy(me, up, z_send.at[0, me], True).start()

    @pl.when(z > 0)
    def _():
        copy(me, down, z_send.at[1, me], True).start()

    spread(me, True)
    own_shard = pltpu.make_async_copy(shard_ref, gathered.at[me], local_sem)
    own_shard.start()

    slots = tiles_ref.shape[0] // nz
    group = min(GROUP, slots)

    def prepare(part):
        @pl.loop(0, slots // group)
        def _(g):
            for u in range(group):
                t = part * slots + g * group + u
                tile = coefficients_ref[t]
                high = tile.astype(jnp.bfloat16).astype(jnp.float32)
                low = tile - high
                first = lax.broadcasted_iota(jnp.int32, tile.shape, 1) < BLK
                even = jnp.where(first, high, pltpu.roll(low, BLK, 1))
                odd = jnp.where(first, pltpu.roll(high, BLK, 1), low)
                tiles_ref[t] = jnp.concatenate([even, odd], axis=0).astype(jnp.bfloat16)

    def from_y(zz):
        if ny > 1:
            q = index(zz, ny - 1 - y, c)
            wait(q)
            copy(q, other_c, c_send.at[q]).start()

    prepare(0)

    @pl.loop(1, nz)
    def _(d):
        @pl.when(z - d >= 0)
        def _():
            q = index(z - d, y, c)
            wait(q)

            @pl.when(z < nz - 1)
            def _():
                copy(q, up, z_send.at[0, q]).start()

            spread(q)

        @pl.when(z + d < nz)
        def _():
            q = index(z + d, y, c)
            wait(q)

            @pl.when(z > 0)
            def _():
                copy(q, down, z_send.at[1, q]).start()

            spread(q)

        prepare(d)

    @pl.loop(0, nz)
    def _(d):
        @pl.when(z - d >= 0)
        def _():
            from_y(z - d)

        @pl.when((z + d < nz) & (d > 0))
        def _():
            from_y(z + d)

    @pl.loop(0, nz * ny)
    def _(j):
        wait(2 * j + 1 - c)

    own_shard.wait()

    @pl.loop(0, nz)
    def _(zz):
        q = index(zz, y, c)

        @pl.when((zz <= z) & (z < nz - 1))
        def _():
            copy(q, up, z_send.at[0, q]).wait_send()

        @pl.when((zz >= z) & (z > 0))
        def _():
            copy(q, down, z_send.at[1, q]).wait_send()

        if ny > 1:
            copy(q, other_y, y_send.at[q]).wait_send()

    @pl.loop(0, nz * ny)
    def _(j):
        q = 2 * j + c
        copy(q, other_c, c_send.at[q]).wait_send()


def exchange_kernel(shape, half_ref, panel_ref, out_ref, arrived, panels, lhs, a_send, a_recv, z_send, y_send, c_send, p_recv, local_sem):
    nz, ny, n = shape
    owned = arrived.shape[1]
    me = lax.axis_index("aux")
    z, y, c = me // (2 * ny), (me // 2) % ny, me % 2

    def index(zz, yy, cc):
        return (zz * ny + yy) * 2 + cc

    def partner(i):
        return lax.rem(i + nz // 2, nz), lax.rem(i // (2 * nz), ny), lax.rem(i // nz, 2)

    def send_to(i):
        k, dy, dc = partner(i)
        return index(lax.rem(z + k, nz), lax.rem(y + dy, ny), lax.rem(c + dc, 2))

    def recv_from(i):
        k, dy, dc = partner(i)
        return index(lax.rem(z - k + nz, nz), lax.rem(y - dy + ny, ny), lax.rem(c - dc + 2, 2))

    barrier = pltpu.get_barrier_semaphore()

    @pl.loop(1, n)
    def _(k):
        pl.semaphore_signal(barrier, inc=1, device_id={"aux": lax.rem(me + k, n)}, device_id_type=MESH_ID)

    pl.semaphore_wait(barrier, n - 1)

    def panel_copy(q, dst, sem, own=False):
        return pltpu.make_async_remote_copy(
            src_ref=panel_ref if own else panels.at[q],
            dst_ref=panels.at[q],
            send_sem=sem,
            recv_sem=p_recv.at[q],
            device_id={"aux": dst},
            device_id_type=MESH_ID,
        )

    def row_copy(dst, slot):
        return pltpu.make_async_remote_copy(
            src_ref=half_ref.at[pl.ds(dst * owned, owned)],
            dst_ref=arrived.at[slot],
            send_sem=a_send.at[dst],
            recv_sem=a_recv.at[slot],
            device_id={"aux": dst},
            device_id_type=MESH_ID,
        )

    def wait_panel(q):
        panel_copy(q, me, c_send.at[q]).wait_recv()

    up, down = index(z + 1, y, c), index(z - 1, y, c)
    other_y, other_c = index(z, ny - 1 - y, c), index(z, y, 1 - c)

    def spread(q, own=False):
        if ny > 1:
            panel_copy(q, other_y, y_send.at[q], own).start()
        panel_copy(q, other_c, c_send.at[q], own).start()

    @pl.when(z < nz - 1)
    def _():
        panel_copy(me, up, z_send.at[0, me], True).start()

    @pl.when(z > 0)
    def _():
        panel_copy(me, down, z_send.at[1, me], True).start()

    spread(me, True)
    own_panel = pltpu.make_async_copy(panel_ref, panels.at[me], local_sem.at[0])
    own_rows = pltpu.make_async_copy(half_ref.at[pl.ds(me * owned, owned)], arrived.at[me], local_sem.at[1])
    own_panel.start()
    own_rows.start()

    batch = n // nz

    def send_rows(part):
        @pl.loop(0, batch)
        def _(j):
            dst = send_to(part * batch + j)

            @pl.when(dst != me)
            def _():
                row_copy(dst, me).start()

    send_rows(0)

    def from_y(zz):
        if ny > 1:
            q = index(zz, ny - 1 - y, c)
            wait_panel(q)
            panel_copy(q, other_c, c_send.at[q]).start()

    def pair_from_y(d):
        @pl.when(z - d >= 0)
        def _():
            from_y(z - d)

        @pl.when((z + d < nz) & (d > 0))
        def _():
            from_y(z + d)

    @pl.loop(1, nz)
    def _(d):
        @pl.when(z - d >= 0)
        def _():
            q = index(z - d, y, c)
            wait_panel(q)

            @pl.when(z < nz - 1)
            def _():
                panel_copy(q, up, z_send.at[0, q]).start()

            spread(q)

        @pl.when(z + d < nz)
        def _():
            q = index(z + d, y, c)
            wait_panel(q)

            @pl.when(z > 0)
            def _():
                panel_copy(q, down, z_send.at[1, q]).start()

            spread(q)

        send_rows(d)
        pair_from_y(d - 1)

    pair_from_y(nz - 1)

    @pl.loop(0, nz * ny)
    def _(j):
        wait_panel(2 * j + 1 - c)

    own_panel.wait()
    own_rows.wait()
    out_ref[...] = jnp.zeros_like(out_ref)
    rows = owned * BLK
    width = out_ref.shape[1]

    @pl.loop(0, n)
    def _(i):
        q = recv_from(i)

        @pl.when(q != me)
        def _():
            row_copy(me, q).wait_recv()

        high, low = halves(arrived[q].reshape(rows, LANES))
        lhs[...] = jnp.concatenate([high, high, low], axis=1)

        @pl.loop(0, width // TILE)
        def _(j):
            start = pl.multiple_of(j * TILE, TILE)
            p_high, p_low = halves(panels[q, :, pl.ds(start, TILE)])
            rhs = jnp.concatenate([p_high, p_low, p_high], axis=0)
            out_ref[:, pl.ds(start, TILE)] += jnp.dot(lhs[...], rhs, preferred_element_type=jnp.float32)

    @pl.loop(0, n)
    def _(i):
        dst = send_to(i)

        @pl.when(dst != me)
        def _():
            row_copy(dst, me).wait_send()

    @pl.loop(0, nz)
    def _(zz):
        q = index(zz, y, c)

        @pl.when((zz <= z) & (z < nz - 1))
        def _():
            panel_copy(q, up, z_send.at[0, q]).wait_send()

        @pl.when((zz >= z) & (z > 0))
        def _():
            panel_copy(q, down, z_send.at[1, q]).wait_send()

        if ny > 1:
            panel_copy(q, other_y, y_send.at[q]).wait_send()

    @pl.loop(0, nz * ny)
    def _(j):
        q = 2 * j + c
        panel_copy(q, other_c, c_send.at[q]).wait_send()


def shards(coefficients, screening, kept_count, occupied, owner_order):
    slot_count = coefficients.shape[1]
    occ = occupied.shape[1]
    n = lax.axis_size("aux")
    shard_rows = occupied.shape[0]
    block_count = shard_rows * n // BLK
    owned = block_count // n
    width = PBLK * BLK
    ny = 2 if n == 16 else 1
    nz = n // (2 * ny)
    dma = pltpu.SemaphoreType.DMA
    place = jnp.zeros((block_count,), jnp.int32).at[owner_order].set(jnp.arange(block_count, dtype=jnp.int32))
    smem = pl.BlockSpec(memory_space=pltpu.SMEM)
    vmem = pl.BlockSpec(memory_space=pltpu.VMEM)
    anyw = pl.BlockSpec(memory_space=pl.ANY)
    flat = BLK * BLK // LANES
    tiles, orbitals = pl.pallas_call(
        functools.partial(spread_kernel, (nz, ny, n)),
        out_shape=(
            jax.ShapeDtypeStruct((slot_count, BLK, LANES), jnp.bfloat16),
            jax.ShapeDtypeStruct((n, shard_rows, LANES), jnp.float32),
        ),
        in_specs=[vmem, anyw],
        out_specs=(vmem, anyw),
        scratch_shapes=[dma((2, n)), dma((n,)), dma((n,)), dma((n,)), dma],
        compiler_params=pltpu.CompilerParams(collective_id=1, has_side_effects=True, vmem_limit_bytes=VMEM_BYTES),
    )(coefficients[0].reshape(slot_count, flat, LANES), jnp.pad(occupied, ((0, 0), (0, LANES - occ))))
    half, panel = pl.pallas_call(
        functools.partial(half_kernel, block_count),
        out_shape=(
            jax.ShapeDtypeStruct((block_count + 1, BLK, LANES), jnp.float32),
            jax.ShapeDtypeStruct((LANES, width), jnp.float32),
        ),
        in_specs=[smem] * 4 + [vmem] * 2,
        out_specs=(vmem, vmem),
        scratch_shapes=[pltpu.VMEM((block_count, 4 * BLK, LANES), jnp.bfloat16)],
        compiler_params=pltpu.CompilerParams(vmem_limit_bytes=VMEM_BYTES),
    )(kept_count, screening[0, 0], screening[1, 0], place, tiles, orbitals.reshape(block_count, BLK, LANES))

    rows = owned * BLK
    out = pl.pallas_call(
        functools.partial(exchange_kernel, (nz, ny, n)),
        out_shape=jax.ShapeDtypeStruct((rows, width), jnp.float32),
        in_specs=[anyw, anyw],
        out_specs=vmem,
        scratch_shapes=[
            pltpu.VMEM((n, owned, BLK, LANES), jnp.float32),
            pltpu.VMEM((n, LANES, width), jnp.float32),
            pltpu.VMEM((rows, 3 * LANES), jnp.bfloat16),
            dma((n,)), dma((n,)), dma((2, n)), dma((n,)), dma((n,)), dma((n,)), dma((2,)),
        ],
        compiler_params=pltpu.CompilerParams(collective_id=0, has_side_effects=True, vmem_limit_bytes=VMEM_BYTES),
    )(half, panel)
    return out.reshape(owned, BLK, width)


def solution(mesh):
    return jax.shard_map(
        shards,
        mesh=mesh,
        in_specs=(
            P(("groups", "aux"), None, None),
            P(None, ("groups", "aux"), None),
            P(("groups", "aux")),
            P(("groups", "aux"), None),
            P("groups"),
        ),
        out_specs=P(("groups", "aux"), None, None),
        check_vma=False,
    )
```
